32 devices in a mesh: sweep: 2 (over x), tp: 8 (over z, y), pp: 2 (over core).
Axes of the slice: x: 2, y: 2, z: 4, core: 2. Of those that a mesh axis runs over, the one named last changes fastest.
Arguments:
- tokens: bfloat16 [256, 8192], P(None, 'tp')
- cotangent: bfloat16 [256, 8192], P(None, 'tp'), may hold values from -6 to 6
- norm_gain: bfloat16 [4, 8192], P(('sweep', 'pp'), 'tp'), parts along dimension 0, may hold values from 0.099609375 to 1.8984375
- gate_band: bfloat16 [4, 64, 2048, 256], P(('sweep', 'pp'), 'tp'), parts along dimension 0, may hold values from -0.125 to 0.125
- up_band: bfloat16 [4, 64, 2048, 256], P(('sweep', 'pp'), 'tp'), parts along dimension 0, may hold values from -0.125 to 0.125
- down_band: bfloat16 [4, 64, 256, 2048], P(('sweep', 'pp'), 'tp'), parts along dimension 0, may hold values from -0.09375 to 0.09375
- offsets: int32 [4, 64], P(('sweep', 'pp'), 'tp'), parts along dimension 0, may hold values from 0 to 31, as said below
- counts: int32 [4], P('sweep'), parts along dimension 0, may hold values from 32 to 128, as said below
Outputs:
- layer_outputs: bfloat16 [4, 256, 8192], P(('sweep', 'pp'), None, 'tp'), parts along dimension 0
- input_grads: bfloat16 [4, 256, 8192], P(('sweep', 'pp'), None, 'tp'), parts along dimension 0
- gate_grads: bfloat16 [4, 64, 2048, 256], P(('sweep', 'pp'), 'tp'), parts along dimension 0
- up_grads: bfloat16 [4, 64, 2048, 256], P(('sweep', 'pp'), 'tp'), parts along dimension 0
- down_grads: bfloat16 [4, 64, 256, 2048], P(('sweep', 'pp'), 'tp'), parts along dimension 0
The draws below stay inside these ranges and needn't reach their ends.
There are 2 independent parts, one for each index of `sweep`. The reference program is written for one: setup_inputs(seed, part) draws one part's arguments, and reference() takes and returns one part's arrays. A program takes and returns all parts, laid end to end along the dimension named above; an argument that names none is the same for every part. Nothing has to cross between parts.
Inputs may be any that keep to these rules, and one draw needn't show every extreme that they name: offsets[l, h] = (h * 8192 // 16384 - 8 // 2 + b) mod (32) with b equal to 0 or 1 for each (l, h). `counts`: the valid tokens of a micro-batch are its first ones; some micro-batch is full.
All inputs are finite; a program needn't handle non-finite values.
Results may differ from the reference program's by a relative error of at most 0.0084.
Values may be sent and summed in bfloat16 or wider, within the bound.
A program may use at most 448 MiB of HBM per device.

```python
import jax
import jax.numpy as jnp
from jax import lax

D = 8192
FF = 16384
BLK = 256
T_MB = 128
MICRO = 2
LAYERS = 2
TOKENS = 256
KB = 8
BAND = 2048
NH = 64


def draw_tokens(key, part):
    sample = jax.random.normal(key, (TOKENS, D), jnp.float32)
    rising = jnp.exp(jnp.log(2.0) * jnp.arange(D, dtype=jnp.float32) / D)
    row_scale = jnp.exp(jax.random.uniform(jax.random.fold_in(key, 7), (TOKENS, 1), jnp.float32, jnp.log(0.5), jnp.log(2.0)))
    return (sample * rising[None, :] * row_scale).astype(jnp.bfloat16)


def draw_offsets(key, part):
    hidden_ids = jnp.arange(FF // BLK, dtype=jnp.int32)
    centre = hidden_ids * (D // BLK) // (FF // BLK)
    shift_bit = jax.random.randint(key, (LAYERS, FF // BLK), 0, 2, jnp.int32)
    ratio = FF // BLK // (D // BLK)
    forced = (hidden_ids == (KB // 2 - 1) * ratio) | (hidden_ids == KB // 2 * ratio)
    shift_bit = jnp.where(forced[None, :], 0, shift_bit)
    return ((centre[None, :] - KB // 2 + shift_bit) % (D // BLK)).astype(jnp.int32)


def draw_counts(key, part):
    drawn = jax.random.randint(key, (MICRO,), T_MB // 4, T_MB, jnp.int32)
    fullest = jax.random.randint(jax.random.fold_in(key, 3), (), 0, MICRO, jnp.int32)
    return jnp.where(jnp.arange(MICRO, dtype=jnp.int32) == fullest, T_MB, drawn).astype(jnp.int32)


def levels(key, dims, pieces, low, largest):
    def one(dim, shards_of):
        draws = jax.random.uniform(jax.random.fold_in(jax.random.fold_in(key, 6), dim), (shards_of,), jnp.float32, low / len(pieces), largest / len(pieces))
        return jnp.repeat(jnp.exp(draws), dims[dim] // shards_of).reshape((-1,) + (1,) * (len(dims) - dim - 1))

    level = one(*pieces[0])
    for cut in pieces[1:]:
        level = level * one(*cut)
    return level


def bell_draw(key, shape, width, bound, shards=(), kind=jnp.bfloat16):
    entries = jax.random.normal(key, shape, jnp.float32) * width
    if len(shards) > 0:
        entries = levels(key, shape, shards, -0.22, 0.18) * entries
    return jnp.clip(entries, min=-bound, max=bound).astype(kind)


def setup_inputs(seed: int = 0, part: int = 0) -> dict:
    arg_keys = jax.random.split(jax.random.key(seed), 9)
    part_splits = jax.random.split(jax.random.fold_in(arg_keys[8], part), 9)
    return {
        "tokens": draw_tokens(jax.random.fold_in(arg_keys[8], 71), part),
        "cotangent": bell_draw(arg_keys[1], (TOKENS, D), 1.0, 6.0, ((1, 8),)),
        "norm_gain": jnp.clip(1.0 + 0.18 * jax.random.normal(part_splits[2], (LAYERS, D), jnp.float32), 0.099609375, 1.8984375).astype(jnp.bfloat16),
        "gate_band": bell_draw(part_splits[3], (LAYERS, NH, BAND, BLK), BAND ** -0.5, 0.125, ((0, 2), (1, 8))),
        "up_band": bell_draw(part_splits[4], (LAYERS, NH, BAND, BLK), BAND ** -0.5, 0.125, ((0, 2), (1, 8))),
        "down_band": bell_draw(part_splits[5], (LAYERS, NH, BLK, BAND), (FF * BAND // D) ** -0.5, 0.09375, ((0, 2), (1, 8))),
        "offsets": draw_offsets(jax.random.fold_in(jax.random.fold_in(arg_keys[8], part), 71), part),
        "counts": draw_counts(jax.random.fold_in(jax.random.fold_in(arg_keys[8], part), 71), part),
    }


EPSILON = 1e-05
HIGH = lax.Precision.HIGHEST

def band_columns(offset_row):
    return ((offset_row[:, None] * BLK + jnp.arange(BAND, dtype=jnp.int32)[None, :]) % D).astype(jnp.int32)

def take_band(matrix, columns):
    rows = matrix.shape[0]
    return jnp.take(matrix, columns.reshape(-1), axis=1).reshape(rows, NH, BAND).astype(jnp.float32)

def spread_band(terms, columns, rows):
    flat_terms = terms.reshape(rows, NH * BAND)
    return jnp.zeros((rows, D), jnp.float32).at[:, columns.reshape(-1)].add(flat_terms)

def layer_forward(layer_in, gain_row, gate_weight, up_weight, down_weight, columns):
    rows = layer_in.shape[0]
    act_f32 = layer_in.astype(jnp.float32)
    inverse = lax.rsqrt(lax.optimization_barrier(jnp.sum(act_f32 * act_f32, axis=1, keepdims=True)) / D + EPSILON)
    normed = (act_f32 * inverse * gain_row.astype(jnp.float32)[None, :]).astype(jnp.bfloat16)
    band_vals = take_band(normed, columns)
    gate_pre = jnp.einsum('thi,hij->thj', band_vals, gate_weight.astype(jnp.float32), precision=HIGH).reshape(rows, FF)
    up_pre = jnp.einsum('thi,hij->thj', band_vals, up_weight.astype(jnp.float32), precision=HIGH).reshape(rows, FF)
    hidden = (jax.nn.silu(gate_pre) * up_pre).astype(jnp.bfloat16)
    terms = jnp.einsum('thj,hji->thi', hidden.reshape(rows, NH, BLK).astype(jnp.float32), down_weight.astype(jnp.float32), precision=HIGH)
    partial_value = spread_band(terms, columns, rows)
    layer_out = (act_f32 + partial_value).astype(jnp.bfloat16)
    return (layer_out, normed, inverse, gate_pre, up_pre, hidden)

def layer_backward(grad_out, layer_in, gain_row, gate_weight, up_weight, down_weight, columns, normed, inverse, gate_pre, up_pre, hidden):
    rows = layer_in.shape[0]
    grad_band = take_band(grad_out, columns)
    hidden_split = hidden.reshape(rows, NH, BLK).astype(jnp.float32)
    grad_hidden = jnp.einsum('thi,hji->thj', grad_band, down_weight.astype(jnp.float32), precision=HIGH).reshape(rows, FF)
    down_grads = jnp.einsum('thj,thi->hji', hidden_split, grad_band, precision=HIGH)
    sigmoid_gate = jax.nn.sigmoid(gate_pre)
    grad_gate = (grad_hidden * up_pre * sigmoid_gate * (1.0 + gate_pre * (1.0 - sigmoid_gate))).astype(jnp.bfloat16)
    grad_up = (grad_hidden * (gate_pre * sigmoid_gate)).astype(jnp.bfloat16)
    gate_split = grad_gate.reshape(rows, NH, BLK).astype(jnp.float32)
    up_split = grad_up.reshape(rows, NH, BLK).astype(jnp.float32)
    band_vals = take_band(normed, columns)
    gate_grads = jnp.einsum('thi,thj->hij', band_vals, gate_split, precision=HIGH)
    up_grads = jnp.einsum('thi,thj->hij', band_vals, up_split, precision=HIGH)
    terms = jnp.einsum('thj,hij->thi', gate_split, gate_weight.astype(jnp.float32), precision=HIGH)
    terms = terms + jnp.einsum('thj,hij->thi', up_split, up_weight.astype(jnp.float32), precision=HIGH)
    grad_normed = spread_band(terms, columns, rows)
    act_f32 = layer_in.astype(jnp.float32)
    normed_f32 = act_f32 * inverse
    scaled = grad_normed * gain_row.astype(jnp.float32)[None, :]
    projection = lax.optimization_barrier(jnp.sum(scaled * normed_f32, axis=1, keepdims=True)) / D
    grad_in = (grad_out.astype(jnp.float32) + inverse * (scaled - normed_f32 * projection)).astype(jnp.bfloat16)
    return (grad_in, gate_grads, up_grads, down_grads)

def reference(tokens, cotangent, norm_gain, gate_band, up_band, down_band, offsets, counts):
    layer_in = tokens
    saved = []
    outputs = []
    for layer_id in range(LAYERS):
        columns = band_columns(offsets[layer_id])
        result = layer_forward(layer_in, norm_gain[layer_id], gate_band[layer_id], up_band[layer_id], down_band[layer_id], columns)
        saved.append((layer_in, columns) + result[1:])
        outputs.append(result[0])
        layer_in = result[0]
    row_ids = jnp.arange(TOKENS, dtype=jnp.int32)
    limits = jnp.repeat(counts, T_MB, total_repeat_length=TOKENS)
    valid_rows = row_ids % T_MB < limits
    grad_out = jnp.where(valid_rows[:, None], cotangent, jnp.zeros((), cotangent.dtype))
    input_list = [None] * LAYERS
    gate_list = [None] * LAYERS
    up_list = [None] * LAYERS
    down_list = [None] * LAYERS
    for layer_id in range(LAYERS - 1, -1, -1):
        layer_in, columns, normed, inverse, gate_pre, up_pre, hidden = saved[layer_id]
        grad_in, gate_grads, up_grads, down_grads = layer_backward(grad_out, layer_in, norm_gain[layer_id], gate_band[layer_id], up_band[layer_id], down_band[layer_id], columns, normed, inverse, gate_pre, up_pre, hidden)
        input_list[layer_id] = grad_in
        gate_list[layer_id] = gate_grads.astype(jnp.bfloat16)
        up_list[layer_id] = up_grads.astype(jnp.bfloat16)
        down_list[layer_id] = down_grads.astype(jnp.bfloat16)
        grad_out = grad_in
    return (jnp.stack(outputs), jnp.stack(input_list), jnp.stack(gate_list), jnp.stack(up_list), jnp.stack(down_list))
```

```python
import functools

import jax
import jax.numpy as jnp
from jax import lax
from jax.experimental import pallas as pl
from jax.experimental.pallas import tpu as pltpu
from jax.sharding import PartitionSpec as P

D = 8192
BLK = 256
T_MB = 128
KB = 8
BAND = 2048
EPSILON = 1e-05
VMEM_LIMIT = 56 * 1024 * 1024
F32 = jnp.float32
BF16 = jnp.bfloat16


def dot(a, b):
    return jnp.dot(a, b, preferred_element_type=F32)


def dot_t(a, b):
    return lax.dot_general(a, b, (((1,), (1,)), ((), ())), preferred_element_type=F32)


def band_of(starts_ref, h):
    return pl.ds(pl.multiple_of(starts_ref[h] * BLK, BLK), BAND)


def fill_normed(normed, act_parts, gain_parts, inverse):
    width = act_parts[0].shape[1]
    for i, (act, gain) in enumerate(zip(act_parts, gain_parts)):
        normed[:, i * width : (i + 1) * width] = (
            act[...].astype(F32) * inverse[...] * gain[...].astype(F32)
        ).astype(BF16)


def emit_parts(total, outs):
    width = outs[0].shape[1]
    for i, out in enumerate(outs):
        out[...] = total[:, i * width : (i + 1) * width].astype(out.dtype)


def stage_kernel(parts, with_forward, with_backward, with_save, starts_ref, *refs):
    refs = list(refs)

    def take(n):
        got = refs[:n]
        del refs[:n]
        return got

    act_parts = take(parts)
    gain_parts = take(parts)
    (inverse,) = take(1)
    grad_parts = take(parts) if with_backward else []
    gate_w, up_w, down_w = take(3)
    forward_outs = take(parts) if with_forward else []
    if with_backward:
        backward_outs = take(parts)
        (projection,) = take(1)
    if with_save:
        hidden_out, gate_out, up_out = take(3)
    (normed,) = take(1)
    if with_forward:
        (forward_total,) = take(1)
    if with_backward:
        grads, backward_total = take(2)

    h = pl.program_id(0)

    @pl.when(h == 0)
    def _():
        fill_normed(normed, act_parts, gain_parts, inverse)
        if with_forward:
            forward_total[...] = jnp.zeros_like(forward_total)
        if with_backward:
            width = grad_parts[0].shape[1]
            for i, grad in enumerate(grad_parts):
                grads[:, i * width : (i + 1) * width] = grad[...]
            backward_total[...] = jnp.zeros_like(backward_total)

    columns = band_of(starts_ref, h)
    band_vals = normed[:, columns]
    gate = dot(band_vals, gate_w[...])
    up = dot(band_vals, up_w[...])
    sig = jax.nn.sigmoid(gate)
    silu = gate * sig
    hidden = (silu * up).astype(BF16)
    if with_forward:
        forward_total[:, columns] += dot(hidden, down_w[...])
    if with_backward:
        grad_hidden = dot_t(grads[:, columns], down_w[...])
        grad_gate = (grad_hidden * up * sig * (1.0 + gate * (1.0 - sig))).astype(BF16)
        grad_up = (grad_hidden * silu).astype(BF16)
        backward_total[:, columns] += dot_t(grad_gate, gate_w[...]) + dot_t(grad_up, up_w[...])
    if with_save:
        hidden_out[...] = hidden
        gate_out[...] = grad_gate
        up_out[...] = grad_up

    @pl.when(h == pl.num_programs(0) - 1)
    def _():
        if with_forward:
            emit_parts(forward_total, forward_outs)
        if with_backward:
            emit_parts(backward_total, backward_outs)
            width = act_parts[0].shape[1]
            products = jnp.zeros((projection.shape[0], 1), F32)
            for i, (act, gain) in enumerate(zip(act_parts, gain_parts)):
                scaled = backward_total[:, i * width : (i + 1) * width] * gain[...].astype(F32)
                products += jnp.sum(
                    scaled * (act[...].astype(F32) * inverse[...]), axis=1, keepdims=True
                )
            projection[...] = products


def whole_spec(array):
    return pl.BlockSpec(array.shape, lambda h, s: (0,) * array.ndim)


def weight_specs():
    return [
        pl.BlockSpec((None, None, BAND, BLK), lambda h, s: (0, h, 0, 0)),
        pl.BlockSpec((None, None, BAND, BLK), lambda h, s: (0, h, 0, 0)),
        pl.BlockSpec((None, None, BLK, BAND), lambda h, s: (0, h, 0, 0)),
    ]


def stage(starts, acts, gains, inverse, grads, weights, with_forward, with_save):
    parts = len(acts)
    reach = parts // 2
    rows, width = acts[0].shape
    hidden_blocks = starts.shape[0]
    with_backward = grads is not None
    ins = list(acts) + list(gains) + [inverse] + (list(grads) if with_backward else [])
    kinds = [F32 if i == reach else BF16 for i in range(parts)]
    shapes = []
    if with_forward:
        shapes += [jax.ShapeDtypeStruct((rows, width), kind) for kind in kinds]
    if with_backward:
        shapes += [jax.ShapeDtypeStruct((rows, width), kind) for kind in kinds]
        shapes += [jax.ShapeDtypeStruct((rows, 1), F32)]
    out_specs = [whole_spec(shape) for shape in shapes]
    if with_save:
        shapes += [jax.ShapeDtypeStruct((rows, hidden_blocks * BLK), BF16)] * 3
        out_specs += [pl.BlockSpec((rows, BLK), lambda h, s: (0, h))] * 3
    scratch = [pltpu.VMEM((rows, parts * width), BF16)]
    if with_forward:
        scratch += [pltpu.VMEM((rows, parts * width), F32)]
    if with_backward:
        scratch += [pltpu.VMEM((rows, parts * width), BF16), pltpu.VMEM((rows, parts * width), F32)]
    products = 2 + (1 if with_forward else 0) + (3 if with_backward else 0)
    return pl.pallas_call(
        functools.partial(stage_kernel, parts, with_forward, with_backward, with_save),
        out_shape=shapes,
        grid_spec=pltpu.PrefetchScalarGridSpec(
            num_scalar_prefetch=1,
            grid=(hidden_blocks,),
            in_specs=[whole_spec(array) for array in ins] + weight_specs(),
            out_specs=out_specs,
            scratch_shapes=scratch,
        ),
        compiler_params=pltpu.CompilerParams(vmem_limit_bytes=VMEM_LIMIT),
        cost_estimate=pl.CostEstimate(
            flops=products * 2 * rows * BAND * BLK * hidden_blocks,
            bytes_accessed=6 * BAND * BLK * hidden_blocks,
            transcendentals=0,
        ),
    )(starts, *ins, *weights)


def weight_kernel(parts, starts_ref, *refs):
    act_parts = refs[:parts]
    gain_parts = refs[parts : 2 * parts]
    inverse = refs[2 * parts]
    grad_parts = refs[2 * parts + 1 : 3 * parts + 1]
    hidden, grad_gate, grad_up = refs[3 * parts + 1 : 3 * parts + 4]
    gate_out, up_out, down_out, normed_t, grads = refs[3 * parts + 4 :]
    h = pl.program_id(0)

    @pl.when(h == 0)
    def _():
        width = act_parts[0].shape[1]
        for i, (act, gain, grad) in enumerate(zip(act_parts, gain_parts, grad_parts)):
            grads[:, i * width : (i + 1) * width] = grad[...]
            normed = (act[...].astype(F32) * inverse[...] * gain[...].astype(F32)).astype(BF16)
            normed_t[i * width : (i + 1) * width, :] = normed.T

    columns = band_of(starts_ref, h)
    band_t = normed_t[columns, :]
    gate_out[...] = dot(band_t, grad_gate[...]).astype(BF16)
    up_out[...] = dot(band_t, grad_up[...]).astype(BF16)
    down_out[...] = dot(hidden[...].T, grads[:, columns]).astype(BF16)


def weight_grads(starts, acts, gains, inverse, grads, saved, weights):
    parts = len(acts)
    rows, width = acts[0].shape
    hidden_blocks = starts.shape[0]
    ins = list(acts) + list(gains) + [inverse] + list(grads)
    return pl.pallas_call(
        functools.partial(weight_kernel, parts),
        out_shape=[jax.ShapeDtypeStruct(w.shape, BF16) for w in weights],
        grid_spec=pltpu.PrefetchScalarGridSpec(
            num_scalar_prefetch=1,
            grid=(hidden_blocks,),
            in_specs=[whole_spec(array) for array in ins]
            + [pl.BlockSpec((rows, BLK), lambda h, s: (0, h))] * 3,
            out_specs=weight_specs(),
            scratch_shapes=[
                pltpu.VMEM((parts * width, rows), BF16),
                pltpu.VMEM((rows, parts * width), BF16),
            ],
        ),
        compiler_params=pltpu.CompilerParams(vmem_limit_bytes=VMEM_LIMIT),
        cost_estimate=pl.CostEstimate(
            flops=6 * rows * BAND * BLK * hidden_blocks,
            bytes_accessed=6 * BAND * BLK * hidden_blocks,
            transcendentals=0,
        ),
    )(starts, *ins, *saved)


def shards(tokens, cotangent, norm_gain, gate_band, up_band, down_band, offsets, counts):
    width = tokens.shape[1]
    blocks_dev = width // BLK
    reach = (KB // 2 - 1 + blocks_dev) // blocks_dev
    section = lax.axis_index("pp")
    position = lax.axis_index("tp")
    count = lax.axis_size("tp")
    sections = lax.axis_size("pp")
    first = section == 0
    starts = jnp.mod(offsets[0] - (position - reach) * blocks_dev, D // BLK)
    weights = (gate_band, up_band, down_band)
    strides = [s for s in range(-reach, reach + 1)]

    def move(value, by, pairs):
        perm = [
            (i * sections + source, (i + by) % count * sections + target)
            for source, target in pairs
            for i in range(count)
        ]
        return lax.ppermute(value, ("tp", "pp"), perm)

    def window(value, pairs):
        return [
            value if s == 0 and pairs[0][0] == pairs[0][1] else move(value, -s, pairs)
            for s in strides
        ]

    def band_sum(pieces, pairs):
        total = pieces[reach]
        for i, s in enumerate(strides):
            if s != 0:
                total = total + move(pieces[i], s, pairs).astype(F32)
        return total

    def choose(a, b):
        return [jnp.where(first, x, y) for x, y in zip(a, b)]

    both = [(0, 0), (1, 1)]
    row_ids = jnp.arange(tokens.shape[0], dtype=jnp.int32)
    valid = row_ids % T_MB < jnp.repeat(counts, T_MB, total_repeat_length=tokens.shape[0])
    cot = jnp.where(valid[:, None], cotangent, jnp.zeros((), BF16))

    own = window(jnp.where(first, tokens, cot), both)
    gains = window(norm_gain, both)
    gain_row = norm_gain.astype(F32)
    tokens_f32 = tokens.astype(F32)
    squares = lax.psum(jnp.sum(tokens_f32 * tokens_f32, axis=1), "tp")
    inverse_0 = lax.rsqrt(squares / D + EPSILON)[:, None]

    pieces = stage(starts, own, gains, inverse_0, None, weights, True, False)
    act_1 = (tokens_f32 + band_sum(pieces, [(0, 0)])).astype(BF16)
    act_1_f32 = act_1.astype(F32)
    squares = lax.psum(
        jnp.where(first, jnp.sum(act_1_f32 * act_1_f32, axis=1), 0.0), ("tp", "pp")
    )
    inverse = jnp.where(first, inverse_0, lax.rsqrt(squares / D + EPSILON)[:, None])
    acts = choose(own, window(act_1, [(0, 1)]))
    layer_in = acts[reach].astype(F32)
    normed = layer_in * inverse

    def input_grad(grad, pieces, projection, pairs):
        scaled = band_sum(pieces, pairs) * gain_row
        return (grad.astype(F32) + inverse * (scaled - normed * (projection / D))).astype(BF16)

    parts = len(strides)
    results = stage(starts, acts, gains, inverse, own, weights, True, False)
    forward_1, backward_1, projection = results[:parts], results[parts : 2 * parts], results[-1]
    projection_1 = lax.psum(projection, "tp")
    grad_1 = input_grad(cot, backward_1, projection_1, [(1, 1)])
    out_1 = (layer_in + band_sum(forward_1, [(1, 1)])).astype(BF16)

    grads = choose(window(grad_1, [(1, 0)]), own)
    results = stage(starts, acts, gains, inverse, grads, weights, False, True)
    backward_0, projection, saved = results[:parts], results[parts], results[parts + 1 :]
    projection_0 = lax.psum(projection, "tp")
    grad_0 = input_grad(grads[reach], backward_0, projection_0, [(0, 0)])
    gate_grads, up_grads, down_grads = weight_grads(
        starts, acts, gains, inverse, grads, saved, weights
    )
    return (
        jnp.where(first, act_1, out_1)[None],
        jnp.where(first, grad_0, grad_1)[None],
        gate_grads,
        up_grads,
        down_grads,
    )


def solution(mesh):
    return jax.shard_map(
        shards,
        mesh=mesh,
        in_specs=(
            P(None, "tp"),
            P(None, "tp"),
            P(("sweep", "pp"), "tp"),
            P(("sweep", "pp"), "tp", None, None),
            P(("sweep", "pp"), "tp", None, None),
            P(("sweep", "pp"), "tp", None, None),
            P(("sweep", "pp"), "tp"),
            P("sweep"),
        ),
        out_specs=(
            P(("sweep", "pp"), None, "tp"),
            P(("sweep", "pp"), None, "tp"),
            P(("sweep", "pp"), "tp", None, None),
            P(("sweep", "pp"), "tp", None, None),
            P(("sweep", "pp"), "tp", None, None),
        ),
        check_vma=False,
    )
```

```python
import functools

import jax
import jax.numpy as jnp
from jax import lax
from jax.experimental import pallas as pl
from jax.experimental.pallas import tpu as pltpu
from jax.sharding import PartitionSpec as P

D = 8192
BLK = 256
T_MB = 128
KB = 8
BAND = 2048
EPSILON = 1e-05
VMEM_LIMIT = 56 * 1024 * 1024
F32 = jnp.float32
BF16 = jnp.bfloat16


def dot(a, b):
    return jnp.dot(a, b, preferred_element_type=F32)


def dot_t(a, b):
    return lax.dot_general(a, b, (((1,), (1,)), ((), ())), preferred_element_type=F32)


def band_of(starts_ref, h):
    return pl.ds(pl.multiple_of(starts_ref[h] * BLK, BLK), BAND)


def fill_normed(normed, act_parts, gain_parts, inverse):
    width = act_parts[0].shape[1]
    for i, (act, gain) in enumerate(zip(act_parts, gain_parts)):
        normed[:, i * width : (i + 1) * width] = (
            act[...].astype(F32) * inverse[...] * gain[0:1, :]
        ).astype(BF16)


def emit_parts(total, outs):
    width = outs[0].shape[1]
    for i, out in enumerate(outs):
        out[...] = total[:, i * width : (i + 1) * width].astype(out.dtype)


def stage_kernel(parts, with_forward, with_backward, with_save, starts_ref, *refs):
    refs = list(refs)

    def take(n):
        got = refs[:n]
        del refs[:n]
        return got

    act_parts = take(parts)
    gain_parts = take(parts)
    (inverse,) = take(1)
    grad_parts = take(parts) if with_backward else []
    gate_w, up_w, down_w = take(3)
    forward_outs = take(parts) if with_forward else []
    if with_backward:
        backward_outs = take(parts)
        (projection,) = take(1)
    if with_save:
        hidden_out, gate_out, up_out = take(3)
    (normed,) = take(1)
    if with_forward:
        (forward_total,) = take(1)
    if with_backward:
        grads, backward_total = take(2)

    h = pl.program_id(0)

    @pl.when(h == 0)
    def _():
        fill_normed(normed, act_parts, gain_parts, inverse)
        if with_forward:
            forward_total[...] = jnp.zeros_like(forward_total)
        if with_backward:
            width = grad_parts[0].shape[1]
            for i, grad in enumerate(grad_parts):
                grads[:, i * width : (i + 1) * width] = grad[...]
            backward_total[...] = jnp.zeros_like(backward_total)

    columns = band_of(starts_ref, h)
    band_vals = normed[:, columns]
    gate = dot(band_vals, gate_w[...])
    up = dot(band_vals, up_w[...])
    sig = jax.nn.sigmoid(gate)
    silu = gate * sig
    hidden = (silu * up).astype(BF16)
    if with_forward:
        forward_total[:, columns] += dot(hidden, down_w[...])
    if with_backward:
        grad_hidden = dot_t(grads[:, columns], down_w[...])
        grad_gate = (grad_hidden * up * sig * (1.0 + gate * (1.0 - sig))).astype(BF16)
        grad_up = (grad_hidden * silu).astype(BF16)
        backward_total[:, columns] += dot_t(grad_gate, gate_w[...]) + dot_t(grad_up, up_w[...])
    if with_save:
        hidden_out[...] = hidden
        gate_out[...] = grad_gate
        up_out[...] = grad_up

    @pl.when(h == pl.num_programs(0) - 1)
    def _():
        if with_forward:
            emit_parts(forward_total, forward_outs)
        if with_backward:
            emit_parts(backward_total, backward_outs)
            width = act_parts[0].shape[1]
            products = jnp.zeros((projection.shape[0], 1), F32)
            for i, (act, gain) in enumerate(zip(act_parts, gain_parts)):
                scaled = backward_total[:, i * width : (i + 1) * width] * gain[0:1, :]
                products += jnp.sum(
                    scaled * (act[...].astype(F32) * inverse[...]), axis=1, keepdims=True
                )
            projection[...] = products


MESH = pl.DeviceIdType.MESH


def to_row(column):
    return jnp.broadcast_to(column, (column.shape[0], 128)).T[0:8, :]


def to_column(row):
    return jnp.broadcast_to(row[0:1, :], (128, row.shape[1])).T[:, 0:1]


def place():
    return lax.axis_index("tp"), lax.axis_index("pp"), lax.axis_size("tp")


def shifted(position, by, count):
    return lax.rem(position + (by % count), count)


def greet():
    position, section, count = place()
    barrier = pltpu.get_barrier_semaphore()
    for j in range(count):
        for other in range(2):
            if j > 0 or other > 0:
                pl.semaphore_signal(
                    barrier,
                    inc=1,
                    device_id={
                        "tp": shifted(position, j, count),
                        "pp": lax.rem(section + other, 2),
                    },
                    device_id_type=MESH,
                )
    pl.semaphore_wait(barrier, 2 * count - 1)


def copies_to(sources, slots, send, recv, strides, section):
    position, _, count = place()
    return [
        pltpu.make_async_remote_copy(
            src_ref=source,
            dst_ref=slots.at[i],
            send_sem=send.at[i],
            recv_sem=recv.at[i],
            device_id={"tp": shifted(position, by, count), "pp": section},
            device_id_type=MESH,
        )
        for i, (source, by) in enumerate(zip(sources, strides))
    ]


def start_all(copies):
    for copy in copies:
        copy.start()


def others(reach):
    return [s for s in range(-reach, reach + 1) if s != 0]


def first_kernel(reach, mine, tokens, gain, *refs):
    parts = 2 * reach + 1
    outs, gain_outs, inverse = refs[:parts], refs[parts : 2 * parts], refs[2 * parts]
    slots, gain_slots, row, rows, s1, r1, s2, r2, s3, r3 = refs[2 * parts + 1 :]
    _, section, count = place()
    strides = [-s for s in others(reach)]
    greet()
    moved = copies_to([mine] * len(strides), slots, s1, r1, strides, section)
    moved_gain = copies_to([gain] * len(strides), gain_slots, s2, r2, strides, section)
    start_all(moved_gain + moved)
    act = tokens[...].astype(F32)
    row[...] = to_row(jnp.sum(act * act, axis=1, keepdims=True))
    moved_row = copies_to([row] * (count - 1), rows, s3, r3, list(range(1, count)), section)
    start_all(moved_row)
    outs[reach][...] = mine[...]
    gain_outs[reach][...] = gain[...]
    for copy in moved_row + moved_gain + moved:
        copy.wait()
    total = row[...]
    for j in range(count - 1):
        total += rows[j]
    inverse[...] = lax.rsqrt(to_column(total) / D + EPSILON)
    for i, s in enumerate(others(reach)):
        outs[reach + s][...] = slots[i]
        gain_outs[reach + s][...] = gain_slots[i]


def act_kernel(reach, *refs):
    parts = 2 * reach + 1
    pieces, own, inverse_0 = refs[:parts], refs[parts : 2 * parts], refs[2 * parts]
    outs, act_1, inverse = refs[2 * parts + 1 : 3 * parts + 1], refs[3 * parts + 1], refs[3 * parts + 2]
    slots, act_slots, row, rows, s1, r1, s2, r2, s3, r3 = refs[3 * parts + 3 :]
    _, section, count = place()
    around = others(reach)
    greet()
    moved = copies_to([pieces[reach + s] for s in around], slots, s1, r1, around, section)
    back = [-s for s in range(-reach, reach + 1)]
    moved_act = copies_to([act_1] * parts, act_slots, s2, r2, back, 1)
    moved_row = copies_to([row] * count, rows, s3, r3, list(range(count)), 1)

    @pl.when(section == 0)
    def _():
        start_all(moved)
        for copy in moved:
            copy.wait()
        total = pieces[reach][...]
        for i in range(len(around)):
            total += slots[i].astype(F32)
        result = (own[reach][...].astype(F32) + total).astype(BF16)
        act_1[...] = result
        start_all(moved_act)
        wide = result.astype(F32)
        row[...] = to_row(jnp.sum(wide * wide, axis=1, keepdims=True))
        start_all(moved_row)
        inverse[...] = inverse_0[...]
        for i in range(parts):
            outs[i][...] = own[i][...]
        for copy in moved_act + moved_row:
            copy.wait_send()

    @pl.when(section != 0)
    def _():
        act_1[...] = jnp.zeros_like(act_1)
        for copy in moved_row + moved_act:
            copy.wait_recv()
        total = rows[0]
        for j in range(1, count):
            total += rows[j]
        inverse[...] = lax.rsqrt(to_column(total) / D + EPSILON)
        for i in range(parts):
            outs[i][...] = act_slots[i]


def grad_kernel(reach, source, hand_on, *refs):
    parts = 2 * reach + 1
    pieces, own = refs[:parts], refs[parts : 2 * parts]
    projection, act, gain, inverse = refs[2 * parts : 2 * parts + 4]
    refs = refs[2 * parts + 4 :]
    outs = ()
    if hand_on:
        outs, refs = refs[:parts], refs[parts:]
    grad, slots, row, rows, s1, r1, s3, r3 = refs[:8]
    _, section, count = place()
    around = others(reach)
    greet()
    moved = copies_to([pieces[reach + s] for s in around], slots, s1, r1, around, section)
    moved_row = copies_to([row] * (count - 1), rows, s3, r3, list(range(1, count)), section)
    if hand_on:
        grad_slots, s2, r2 = refs[8:]
        back = [-s for s in range(-reach, reach + 1)]
        moved_grad = copies_to([grad] * parts, grad_slots, s2, r2, back, 1 - source)

    @pl.when(section == source)
    def _():
        start_all(moved)
        row[...] = to_row(projection[...])
        start_all(moved_row)
        for copy in moved_row + moved:
            copy.wait()
        summed = row[...]
        for j in range(count - 1):
            summed += rows[j]
        total = pieces[reach][...]
        for i in range(len(around)):
            total += slots[i].astype(F32)
        scale = inverse[...]
        normed = act[...].astype(F32) * scale
        mean = to_column(summed) / D
        grad[...] = (
            own[reach][...].astype(F32) + scale * (total * gain[0:1, :] - normed * mean)
        ).astype(BF16)
        if hand_on:
            start_all(moved_grad)
            for i in range(parts):
                outs[i][...] = own[i][...]
            for copy in moved_grad:
                copy.wait_send()

    @pl.when(section != source)
    def _():
        grad[...] = jnp.zeros_like(grad)
        if hand_on:
            for copy in moved_grad:
                copy.wait_recv()
            for i in range(parts):
                outs[i][...] = grad_slots[i]


def sems(*counts):
    return [pltpu.SemaphoreType.DMA((n,)) for n in counts for _ in range(2)]


def linked(kernel, identity, ins, shapes, scratch):
    vmem = pl.BlockSpec(memory_space=pltpu.VMEM)
    return pl.pallas_call(
        kernel,
        out_shape=shapes,
        in_specs=[vmem] * len(ins),
        out_specs=[vmem] * len(shapes),
        scratch_shapes=scratch,
        compiler_params=pltpu.CompilerParams(
            collective_id=identity, has_side_effects=True, vmem_limit_bytes=VMEM_LIMIT
        ),
    )(*ins)


def whole_spec(array):
    return pl.BlockSpec(array.shape, lambda h, s: (0,) * array.ndim)


def weight_specs():
    return [
        pl.BlockSpec((None, None, BAND, BLK), lambda h, s: (0, h, 0, 0)),
        pl.BlockSpec((None, None, BAND, BLK), lambda h, s: (0, h, 0, 0)),
        pl.BlockSpec((None, None, BLK, BAND), lambda h, s: (0, h, 0, 0)),
    ]


def stage(starts, acts, gains, inverse, grads, weights, with_forward, with_save):
    parts = len(acts)
    reach = parts // 2
    rows, width = acts[0].shape
    hidden_blocks = starts.shape[0]
    with_backward = grads is not None
    ins = list(acts) + list(gains) + [inverse] + (list(grads) if with_backward else [])
    kinds = [F32 if i == reach else BF16 for i in range(parts)]
    shapes = []
    if with_forward:
        shapes += [jax.ShapeDtypeStruct((rows, width), kind) for kind in kinds]
    if with_backward:
        shapes += [jax.ShapeDtypeStruct((rows, width), kind) for kind in kinds]
        shapes += [jax.ShapeDtypeStruct((rows, 1), F32)]
    out_specs = [whole_spec(shape) for shape in shapes]
    if with_save:
        shapes += [jax.ShapeDtypeStruct((rows, hidden_blocks * BLK), BF16)] * 3
        out_specs += [pl.BlockSpec((rows, BLK), lambda h, s: (0, h))] * 3
    scratch = [pltpu.VMEM((rows, parts * width), BF16)]
    if with_forward:
        scratch += [pltpu.VMEM((rows, parts * width), F32)]
    if with_backward:
        scratch += [pltpu.VMEM((rows, parts * width), BF16), pltpu.VMEM((rows, parts * width), F32)]
    products = 2 + (1 if with_forward else 0) + (3 if with_backward else 0)
    return pl.pallas_call(
        functools.partial(stage_kernel, parts, with_forward, with_backward, with_save),
        out_shape=shapes,
        grid_spec=pltpu.PrefetchScalarGridSpec(
            num_scalar_prefetch=1,
            grid=(hidden_blocks,),
            in_specs=[whole_spec(array) for array in ins] + weight_specs(),
            out_specs=out_specs,
            scratch_shapes=scratch,
        ),
        compiler_params=pltpu.CompilerParams(vmem_limit_bytes=VMEM_LIMIT),
        cost_estimate=pl.CostEstimate(
            flops=products * 2 * rows * BAND * BLK * hidden_blocks,
            bytes_accessed=6 * BAND * BLK * hidden_blocks,
            transcendentals=0,
        ),
    )(starts, *ins, *weights)


def weight_kernel(parts, starts_ref, *refs):
    act_parts = refs[:parts]
    gain_parts = refs[parts : 2 * parts]
    inverse = refs[2 * parts]
    grad_parts = refs[2 * parts + 1 : 3 * parts + 1]
    hidden, grad_gate, grad_up = refs[3 * parts + 1 : 3 * parts + 4]
    gate_out, up_out, down_out, normed_t, grads = refs[3 * parts + 4 :]
    h = pl.program_id(0)

    @pl.when(h == 0)
    def _():
        width = act_parts[0].shape[1]
        for i, (act, gain, grad) in enumerate(zip(act_parts, gain_parts, grad_parts)):
            grads[:, i * width : (i + 1) * width] = grad[...]
            normed = (act[...].astype(F32) * inverse[...] * gain[0:1, :]).astype(BF16)
            normed_t[i * width : (i + 1) * width, :] = normed.T

    columns = band_of(starts_ref, h)
    band_t = normed_t[columns, :]
    gate_out[...] = dot(band_t, grad_gate[...]).astype(BF16)
    up_out[...] = dot(band_t, grad_up[...]).astype(BF16)
    down_out[...] = dot(hidden[...].T, grads[:, columns]).astype(BF16)


def weight_grads(starts, acts, gains, inverse, grads, saved, weights):
    parts = len(acts)
    rows, width = acts[0].shape
    hidden_blocks = starts.shape[0]
    ins = list(acts) + list(gains) + [inverse] + list(grads)
    return pl.pallas_call(
        functools.partial(weight_kernel, parts),
        out_shape=[jax.ShapeDtypeStruct(w.shape, BF16) for w in weights],
        grid_spec=pltpu.PrefetchScalarGridSpec(
            num_scalar_prefetch=1,
            grid=(hidden_blocks,),
            in_specs=[whole_spec(array) for array in ins]
            + [pl.BlockSpec((rows, BLK), lambda h, s: (0, h))] * 3,
            out_specs=weight_specs(),
            scratch_shapes=[
                pltpu.VMEM((parts * width, rows), BF16),
                pltpu.VMEM((rows, parts * width), BF16),
            ],
        ),
        compiler_params=pltpu.CompilerParams(vmem_limit_bytes=VMEM_LIMIT),
        cost_estimate=pl.CostEstimate(
            flops=6 * rows * BAND * BLK * hidden_blocks,
            bytes_accessed=6 * BAND * BLK * hidden_blocks,
            transcendentals=0,
        ),
    )(starts, *ins, *saved)


def shards(tokens, cotangent, norm_gain, gate_band, up_band, down_band, offsets, counts):
    width = tokens.shape[1]
    blocks_dev = width // BLK
    reach = (KB // 2 - 1 + blocks_dev) // blocks_dev
    section = lax.axis_index("pp")
    position = lax.axis_index("tp")
    count = lax.axis_size("tp")
    sections = lax.axis_size("pp")
    first = section == 0
    starts = jnp.mod(offsets[0] - (position - reach) * blocks_dev, D // BLK)
    weights = (gate_band, up_band, down_band)
    strides = [s for s in range(-reach, reach + 1)]

    def move(value, by, pairs):
        perm = [
            (i * sections + source, (i + by) % count * sections + target)
            for source, target in pairs
            for i in range(count)
        ]
        return lax.ppermute(value, ("tp", "pp"), perm)

    def band_sum(pieces, pairs):
        total = pieces[reach]
        for i, s in enumerate(strides):
            if s != 0:
                total = total + move(pieces[i], s, pairs).astype(F32)
        return total

    row_ids = jnp.arange(tokens.shape[0], dtype=jnp.int32)
    valid = row_ids % T_MB < jnp.repeat(counts, T_MB, total_repeat_length=tokens.shape[0])
    cot = jnp.where(valid[:, None], cotangent, jnp.zeros((), BF16))

    rows = tokens.shape[0]
    parts = len(strides)
    near = parts - 1
    block = jax.ShapeDtypeStruct((rows, width), BF16)
    column = jax.ShapeDtypeStruct((rows, 1), F32)
    gain = jnp.broadcast_to(norm_gain.astype(F32), (8, width))
    gain_shape = jax.ShapeDtypeStruct(gain.shape, F32)

    def blocks(n):
        return pltpu.VMEM((n, rows, width), BF16)

    def stats(n):
        return [pltpu.VMEM((8, rows), F32), pltpu.VMEM((n, 8, rows), F32)]

    results = linked(
        functools.partial(first_kernel, reach),
        0,
        [jnp.where(first, tokens, cot), tokens, gain],
        [block] * parts + [gain_shape] * parts + [column],
        [blocks(near), pltpu.VMEM((near, 8, width), F32)]
        + stats(count - 1)
        + sems(near, near, count - 1),
    )
    own, gains, inverse_0 = results[:parts], results[parts : 2 * parts], results[-1]

    pieces = stage(starts, own, gains, inverse_0, None, weights, True, False)
    results = linked(
        functools.partial(act_kernel, reach),
        1,
        [*pieces, *own, inverse_0],
        [block] * parts + [block, column],
        [blocks(near), blocks(parts)] + stats(count) + sems(near, parts, count),
    )
    acts, act_1, inverse = results[:parts], results[parts], results[parts + 1]

    results = stage(starts, acts, gains, inverse, own, weights, True, False)
    forward_1, backward_1, projection = results[:parts], results[parts : 2 * parts], results[-1]
    results = linked(
        functools.partial(grad_kernel, reach, 1, True),
        2,
        [*backward_1, *own, projection, acts[reach], gain, inverse],
        [block] * parts + [block],
        [blocks(near)]
        + stats(count - 1)
        + sems(near, count - 1)
        + [blocks(parts)]
        + sems(parts),
    )
    grads, grad_1 = results[:parts], results[parts]
    out_1 = (acts[reach].astype(F32) + band_sum(forward_1, [(1, 1)])).astype(BF16)

    results = stage(starts, acts, gains, inverse, grads, weights, False, True)
    backward_0, projection, saved = results[:parts], results[parts], results[parts + 1 :]
    (grad_0,) = linked(
        functools.partial(grad_kernel, reach, 0, False),
        3,
        [*backward_0, *grads, projection, acts[reach], gain, inverse],
        [block],
        [blocks(near)] + stats(count - 1) + sems(near, count - 1),
    )
    gate_grads, up_grads, down_grads = weight_grads(
        starts, acts, gains, inverse, grads, saved, weights
    )
    return (
        jnp.where(first, act_1, out_1)[None],
        jnp.where(first, grad_0, grad_1)[None],
        gate_grads,
        up_grads,
        down_grads,
    )


def solution(mesh):
    return jax.shard_map(
        shards,
        mesh=mesh,
        in_specs=(
            P(None, "tp"),
            P(None, "tp"),
            P(("sweep", "pp"), "tp"),
            P(("sweep", "pp"), "tp", None, None),
            P(("sweep", "pp"), "tp", None, None),
            P(("sweep", "pp"), "tp", None, None),
            P(("sweep", "pp"), "tp"),
            P("sweep"),
        ),
        out_specs=(
            P(("sweep", "pp"), None, "tp"),
            P(("sweep", "pp"), None, "tp"),
            P(("sweep", "pp"), "tp", None, None),
            P(("sweep", "pp"), "tp", None, None),
            P(("sweep", "pp"), "tp", None, None),
        ),
        check_vma=False,
    )
```

```python
import functools

import jax
import jax.numpy as jnp
from jax import lax
from jax.experimental import pallas as pl
from jax.experimental.pallas import tpu as pltpu
from jax.sharding import PartitionSpec as P

D = 8192
BLK = 256
T_MB = 128
KB = 8
BAND = 2048
EPSILON = 1e-05
VMEM_LIMIT = 56 * 1024 * 1024
F32 = jnp.float32
BF16 = jnp.bfloat16


def dot(a, b):
    return jnp.dot(a, b, preferred_element_type=F32)


def dot_t(a, b):
    return lax.dot_general(a, b, (((1,), (1,)), ((), ())), preferred_element_type=F32)


def band_of(starts_ref, h):
    return pl.ds(pl.multiple_of(starts_ref[h] * BLK, BLK), BAND)


def fill_normed(normed, act_parts, gain_parts, inverse):
    width = act_parts[0].shape[1]
    for i, (act, gain) in enumerate(zip(act_parts, gain_parts)):
        normed[:, i * width : (i + 1) * width] = (
            act[...].astype(F32) * inverse[...] * gain[0:1, :]
        ).astype(BF16)


def emit_parts(total, outs):
    width = outs[0].shape[1]
    for i, out in enumerate(outs):
        out[...] = total[:, i * width : (i + 1) * width].astype(out.dtype)


def stage_kernel(parts, with_forward, with_backward, with_save, starts_ref, *refs):
    refs = list(refs)

    def take(n):
        got = refs[:n]
        del refs[:n]
        return got

    act_parts = take(parts)
    gain_parts = take(parts)
    (inverse,) = take(1)
    grad_parts = take(parts) if with_backward else []
    gate_w, up_w, down_w = take(3)
    forward_outs = take(parts) if with_forward else []
    if with_backward:
        backward_outs = take(parts)
        (projection,) = take(1)
    if with_save:
        hidden_out, gate_out, up_out = take(3)
    (normed,) = take(1)
    if with_forward:
        (forward_total,) = take(1)
    if with_backward:
        grads, backward_total = take(2)

    h = pl.program_id(0)

    @pl.when(h == 0)
    def _():
        fill_normed(normed, act_parts, gain_parts, inverse)
        if with_forward:
            forward_total[...] = jnp.zeros_like(forward_total)
        if with_backward:
            width = grad_parts[0].shape[1]
            for i, grad in enumerate(grad_parts):
                grads[:, i * width : (i + 1) * width] = grad[...]
            backward_total[...] = jnp.zeros_like(backward_total)

    columns = band_of(starts_ref, h)
    band_vals = normed[:, columns]
    gate = dot(band_vals, gate_w[...])
    up = dot(band_vals, up_w[...])
    sig = jax.nn.sigmoid(gate)
    silu = gate * sig
    hidden = (silu * up).astype(BF16)
    if with_forward:
        forward_total[:, columns] += dot(hidden, down_w[...])
    if with_backward:
        grad_hidden = dot_t(grads[:, columns], down_w[...])
        grad_gate = (grad_hidden * up * sig * (1.0 + gate * (1.0 - sig))).astype(BF16)
        grad_up = (grad_hidden * silu).astype(BF16)
        backward_total[:, columns] += dot_t(grad_gate, gate_w[...]) + dot_t(grad_up, up_w[...])
    if with_save:
        hidden_out[...] = hidden
        gate_out[...] = grad_gate
        up_out[...] = grad_up

    @pl.when(h == pl.num_programs(0) - 1)
    def _():
        if with_forward:
            emit_parts(forward_total, forward_outs)
        if with_backward:
            emit_parts(backward_total, backward_outs)
            width = act_parts[0].shape[1]
            products = jnp.zeros((projection.shape[0], 1), F32)
            for i, (act, gain) in enumerate(zip(act_parts, gain_parts)):
                scaled = backward_total[:, i * width : (i + 1) * width] * gain[0:1, :]
                products += jnp.sum(
                    scaled * (act[...].astype(F32) * inverse[...]), axis=1, keepdims=True
                )
            projection[...] = products


MESH = pl.DeviceIdType.MESH


def to_row(column):
    return jnp.broadcast_to(column, (column.shape[0], 128)).T[0:8, :]


def to_column(row):
    return jnp.broadcast_to(row[0:1, :], (128, row.shape[1])).T[:, 0:1]


def place():
    return lax.axis_index("tp"), lax.axis_index("pp"), lax.axis_size("tp")


def shifted(position, by, count):
    return lax.rem(position + (by % count), count)


def greet():
    position, section, count = place()
    barrier = pltpu.get_barrier_semaphore()
    for j in range(count):
        for other in range(2):
            if j > 0 or other > 0:
                pl.semaphore_signal(
                    barrier,
                    inc=1,
                    device_id={
                        "tp": shifted(position, j, count),
                        "pp": lax.rem(section + other, 2),
                    },
                    device_id_type=MESH,
                )
    pl.semaphore_wait(barrier, 2 * count - 1)


def copies_to(sources, slots, send, recv, strides, section):
    position, _, count = place()
    return [
        pltpu.make_async_remote_copy(
            src_ref=source,
            dst_ref=slots.at[i],
            send_sem=send.at[i],
            recv_sem=recv.at[i],
            device_id={"tp": shifted(position, by, count), "pp": section},
            device_id_type=MESH,
        )
        for i, (source, by) in enumerate(zip(sources, strides))
    ]


def start_all(copies):
    for copy in copies:
        copy.start()


def others(reach):
    return [s for s in range(-reach, reach + 1) if s != 0]


def first_kernel(reach, tokens, gain, *refs):
    parts = 2 * reach + 1
    outs, gain_outs, inverse = refs[:parts], refs[parts : 2 * parts], refs[2 * parts]
    slots, gain_slots, row, rows, s1, r1, s2, r2, s3, r3 = refs[2 * parts + 1 :]
    _, section, count = place()
    strides = [-s for s in others(reach)]
    greet()
    moved = copies_to([tokens] * len(strides), slots, s1, r1, strides, section)
    moved_gain = copies_to([gain] * len(strides), gain_slots, s2, r2, strides, section)
    moved_row = copies_to([row] * (count - 1), rows, s3, r3, list(range(1, count)), section)
    start_all(moved_gain)
    outs[reach][...] = tokens[...]
    gain_outs[reach][...] = gain[...]

    @pl.when(section == 0)
    def _():
        start_all(moved)
        act = tokens[...].astype(F32)
        row[...] = to_row(jnp.sum(act * act, axis=1, keepdims=True))
        start_all(moved_row)
        for copy in moved_row + moved:
            copy.wait()
        total = row[...]
        for j in range(count - 1):
            total += rows[j]
        inverse[...] = lax.rsqrt(to_column(total) / D + EPSILON)
        for i, s in enumerate(others(reach)):
            outs[reach + s][...] = slots[i]

    @pl.when(section != 0)
    def _():
        inverse[...] = jnp.zeros_like(inverse)
        for s in others(reach):
            outs[reach + s][...] = jnp.zeros_like(outs[reach + s])

    for copy in moved_gain:
        copy.wait()
    for i, s in enumerate(others(reach)):
        gain_outs[reach + s][...] = gain_slots[i]


def sum_kernel(projection, summed, row, rows, send, recv):
    _, section, count = place()
    greet()
    row[...] = to_row(projection[...])
    moved = copies_to([row] * (count - 1), rows, send, recv, list(range(1, count)), section)
    start_all(moved)
    for copy in moved:
        copy.wait()
    total = row[...]
    for j in range(count - 1):
        total += rows[j]
    summed[...] = to_column(total)


def act_kernel(reach, *refs):
    parts = 2 * reach + 1
    pieces, own, inverse_0 = refs[:parts], refs[parts : 2 * parts], refs[2 * parts]
    outs, act_1, inverse = refs[2 * parts + 1 : 3 * parts + 1], refs[3 * parts + 1], refs[3 * parts + 2]
    slots, act_slots, row, rows, s1, r1, s2, r2, s3, r3 = refs[3 * parts + 3 :]
    _, section, count = place()
    around = others(reach)
    greet()
    moved = copies_to([pieces[reach + s] for s in around], slots, s1, r1, around, section)
    back = [-s for s in range(-reach, reach + 1)]
    moved_act = copies_to([act_1] * parts, act_slots, s2, r2, back, 1)
    moved_row = copies_to([row] * count, rows, s3, r3, list(range(count)), 1)

    @pl.when(section == 0)
    def _():
        start_all(moved)
        for copy in moved:
            copy.wait()
        total = pieces[reach][...]
        for i in range(len(around)):
            total += slots[i].astype(F32)
        result = (own[reach][...].astype(F32) + total).astype(BF16)
        act_1[...] = result
        start_all(moved_act)
        wide = result.astype(F32)
        row[...] = to_row(jnp.sum(wide * wide, axis=1, keepdims=True))
        start_all(moved_row)
        inverse[...] = inverse_0[...]
        for i in range(parts):
            outs[i][...] = own[i][...]
        for copy in moved_act + moved_row:
            copy.wait_send()

    @pl.when(section != 0)
    def _():
        act_1[...] = jnp.zeros_like(act_1)
        for copy in moved_row + moved_act:
            copy.wait_recv()
        total = rows[0]
        for j in range(1, count):
            total += rows[j]
        inverse[...] = lax.rsqrt(to_column(total) / D + EPSILON)
        for i in range(parts):
            outs[i][...] = act_slots[i]


def grad_kernel(reach, source, hand_on, *refs):
    parts = 2 * reach + 1
    pieces, own = refs[:parts], refs[parts : 2 * parts]
    projection, act, gain, inverse = refs[2 * parts : 2 * parts + 4]
    refs = refs[2 * parts + 4 :]
    outs = ()
    if hand_on:
        outs, refs = refs[:parts], refs[parts:]
    grad, slots, row, rows, s1, r1, s3, r3 = refs[:8]
    _, section, count = place()
    around = others(reach)
    greet()
    moved = copies_to([pieces[reach + s] for s in around], slots, s1, r1, around, section)
    moved_row = copies_to([row] * (count - 1), rows, s3, r3, list(range(1, count)), section)
    if hand_on:
        grad_slots, s2, r2 = refs[8:]
        back = [-s for s in range(-reach, reach + 1)]
        moved_grad = copies_to([grad] * parts, grad_slots, s2, r2, back, 1 - source)

    @pl.when(section == source)
    def _():
        start_all(moved)
        row[...] = to_row(projection[...])
        start_all(moved_row)
        for copy in moved_row + moved:
            copy.wait()
        summed = row[...]
        for j in range(count - 1):
            summed += rows[j]
        total = pieces[reach][...]
        for i in range(len(around)):
            total += slots[i].astype(F32)
        scale = inverse[...]
        normed = act[...].astype(F32) * scale
        mean = to_column(summed) / D
        grad[...] = (
            own[reach][...].astype(F32) + scale * (total * gain[0:1, :] - normed * mean)
        ).astype(BF16)
        if hand_on:
            start_all(moved_grad)
            for i in range(parts):
                outs[i][...] = own[i][...]
            for copy in moved_grad:
                copy.wait_send()

    @pl.when(section != source)
    def _():
        grad[...] = jnp.zeros_like(grad)
        if hand_on:
            for copy in moved_grad:
                copy.wait_recv()
            for i in range(parts):
                outs[i][...] = grad_slots[i]


def sems(*counts):
    return [pltpu.SemaphoreType.DMA((n,)) for n in counts for _ in range(2)]


def linked(kernel, identity, ins, shapes, scratch):
    vmem = pl.BlockSpec(memory_space=pltpu.VMEM)
    return pl.pallas_call(
        kernel,
        out_shape=shapes,
        in_specs=[vmem] * len(ins),
        out_specs=[vmem] * len(shapes),
        scratch_shapes=scratch,
        compiler_params=pltpu.CompilerParams(
            collective_id=identity, has_side_effects=True, vmem_limit_bytes=VMEM_LIMIT
        ),
    )(*ins)


def whole_spec(array):
    return pl.BlockSpec(array.shape, lambda h, s: (0,) * array.ndim)


def weight_specs():
    return [
        pl.BlockSpec((None, None, BAND, BLK), lambda h, s: (0, h, 0, 0)),
        pl.BlockSpec((None, None, BAND, BLK), lambda h, s: (0, h, 0, 0)),
        pl.BlockSpec((None, None, BLK, BAND), lambda h, s: (0, h, 0, 0)),
    ]


def stage(starts, acts, gains, inverse, grads, weights, with_forward, with_save):
    parts = len(acts)
    reach = parts // 2
    rows, width = acts[0].shape
    hidden_blocks = starts.shape[0]
    with_backward = grads is not None
    ins = list(acts) + list(gains) + [inverse] + (list(grads) if with_backward else [])
    kinds = [F32 if i == reach else BF16 for i in range(parts)]
    shapes = []
    if with_forward:
        shapes += [jax.ShapeDtypeStruct((rows, width), kind) for kind in kinds]
    if with_backward:
        shapes += [jax.ShapeDtypeStruct((rows, width), kind) for kind in kinds]
        shapes += [jax.ShapeDtypeStruct((rows, 1), F32)]
    out_specs = [whole_spec(shape) for shape in shapes]
    if with_save:
        shapes += [jax.ShapeDtypeStruct((rows, hidden_blocks * BLK), BF16)] * 3
        out_specs += [pl.BlockSpec((rows, BLK), lambda h, s: (0, h))] * 3
    scratch = [pltpu.VMEM((rows, parts * width), BF16)]
    if with_forward:
        scratch += [pltpu.VMEM((rows, parts * width), F32)]
    if with_backward:
        scratch += [pltpu.VMEM((rows, parts * width), BF16), pltpu.VMEM((rows, parts * width), F32)]
    products = 2 + (1 if with_forward else 0) + (3 if with_backward else 0)
    return pl.pallas_call(
        functools.partial(stage_kernel, parts, with_forward, with_backward, with_save),
        out_shape=shapes,
        grid_spec=pltpu.PrefetchScalarGridSpec(
            num_scalar_prefetch=1,
            grid=(hidden_blocks,),
            in_specs=[whole_spec(array) for array in ins] + weight_specs(),
            out_specs=out_specs,
            scratch_shapes=scratch,
        ),
        compiler_params=pltpu.CompilerParams(vmem_limit_bytes=VMEM_LIMIT),
        cost_estimate=pl.CostEstimate(
            flops=products * 2 * rows * BAND * BLK * hidden_blocks,
            bytes_accessed=6 * BAND * BLK * hidden_blocks,
            transcendentals=0,
        ),
    )(starts, *ins, *weights)


def weight_kernel(parts, starts_ref, *refs):
    act_parts = refs[:parts]
    gain_parts = refs[parts : 2 * parts]
    inverse = refs[2 * parts]
    grad_parts = refs[2 * parts + 1 : 3 * parts + 1]
    hidden, grad_gate, grad_up = refs[3 * parts + 1 : 3 * parts + 4]
    gate_out, up_out, down_out, normed_t, grads = refs[3 * parts + 4 :]
    h = pl.program_id(0)

    @pl.when(h == 0)
    def _():
        width = act_parts[0].shape[1]
        for i, (act, gain, grad) in enumerate(zip(act_parts, gain_parts, grad_parts)):
            grads[:, i * width : (i + 1) * width] = grad[...]
            normed = (act[...].astype(F32) * inverse[...] * gain[0:1, :]).astype(BF16)
            normed_t[i * width : (i + 1) * width, :] = normed.T

    columns = band_of(starts_ref, h)
    band_t = normed_t[columns, :]
    gate_out[...] = dot(band_t, grad_gate[...]).astype(BF16)
    up_out[...] = dot(band_t, grad_up[...]).astype(BF16)
    down_out[...] = dot(hidden[...].T, grads[:, columns]).astype(BF16)


def weight_grads(starts, acts, gains, inverse, grads, saved, weights):
    parts = len(acts)
    rows, width = acts[0].shape
    hidden_blocks = starts.shape[0]
    ins = list(acts) + list(gains) + [inverse] + list(grads)
    return pl.pallas_call(
        functools.partial(weight_kernel, parts),
        out_shape=[jax.ShapeDtypeStruct(w.shape, BF16) for w in weights],
        grid_spec=pltpu.PrefetchScalarGridSpec(
            num_scalar_prefetch=1,
            grid=(hidden_blocks,),
            in_specs=[whole_spec(array) for array in ins]
            + [pl.BlockSpec((rows, BLK), lambda h, s: (0, h))] * 3,
            out_specs=weight_specs(),
            scratch_shapes=[
                pltpu.VMEM((parts * width, rows), BF16),
                pltpu.VMEM((rows, parts * width), BF16),
            ],
        ),
        compiler_params=pltpu.CompilerParams(vmem_limit_bytes=VMEM_LIMIT),
        cost_estimate=pl.CostEstimate(
            flops=6 * rows * BAND * BLK * hidden_blocks,
            bytes_accessed=6 * BAND * BLK * hidden_blocks,
            transcendentals=0,
        ),
    )(starts, *ins, *saved)


def shards(tokens, cotangent, norm_gain, gate_band, up_band, down_band, offsets, counts):
    width = tokens.shape[1]
    blocks_dev = width // BLK
    reach = (KB // 2 - 1 + blocks_dev) // blocks_dev
    section = lax.axis_index("pp")
    position = lax.axis_index("tp")
    count = lax.axis_size("tp")
    sections = lax.axis_size("pp")
    first = section == 0
    starts = jnp.mod(offsets[0] - (position - reach) * blocks_dev, D // BLK)
    weights = (gate_band, up_band, down_band)
    strides = [s for s in range(-reach, reach + 1)]

    def move(value, by, pairs):
        perm = [
            (i * sections + source, (i + by) % count * sections + target)
            for source, target in pairs
            for i in range(count)
        ]
        return lax.ppermute(value, ("tp", "pp"), perm)

    def band_sum(pieces, pairs):
        total = pieces[reach]
        for i, s in enumerate(strides):
            if s != 0:
                total = total + move(pieces[i], s, pairs).astype(F32)
        return total

    row_ids = jnp.arange(tokens.shape[0], dtype=jnp.int32)
    valid = row_ids % T_MB < jnp.repeat(counts, T_MB, total_repeat_length=tokens.shape[0])
    cot = jnp.where(valid[:, None], cotangent, jnp.zeros((), BF16))

    rows = tokens.shape[0]
    parts = len(strides)
    near = parts - 1
    block = jax.ShapeDtypeStruct((rows, width), BF16)
    column = jax.ShapeDtypeStruct((rows, 1), F32)
    gain = jnp.broadcast_to(norm_gain.astype(F32), (8, width))
    gain_shape = jax.ShapeDtypeStruct(gain.shape, F32)

    def blocks(n):
        return pltpu.VMEM((n, rows, width), BF16)

    def stats(n):
        return [pltpu.VMEM((8, rows), F32), pltpu.VMEM((n, 8, rows), F32)]

    results = linked(
        functools.partial(first_kernel, reach),
        0,
        [tokens, gain],
        [block] * parts + [gain_shape] * parts + [column],
        [blocks(near), pltpu.VMEM((near, 8, width), F32)]
        + stats(count - 1)
        + sems(near, near, count - 1),
    )
    acts_0, gains, inverse_0 = results[:parts], results[parts : 2 * parts], results[-1]
    late_cot, inverse_0 = lax.optimization_barrier((cot, inverse_0))
    own = [cot if s == 0 else move(late_cot, -s, [(1, 1)]) for s in strides]

    pieces = stage(starts, acts_0, gains, inverse_0, None, weights, True, False)
    results = linked(
        functools.partial(act_kernel, reach),
        1,
        [*pieces, *acts_0, inverse_0],
        [block] * parts + [block, column],
        [blocks(near), blocks(parts)] + stats(count) + sems(near, parts, count),
    )
    acts, act_1, inverse = results[:parts], results[parts], results[parts + 1]

    results = stage(starts, acts, gains, inverse, own, weights, True, False)
    forward_1, backward_1, projection = results[:parts], results[parts : 2 * parts], results[-1]
    results = linked(
        functools.partial(grad_kernel, reach, 1, True),
        2,
        [*backward_1, *own, projection, acts[reach], gain, inverse],
        [block] * parts + [block],
        [blocks(near)]
        + stats(count - 1)
        + sems(near, count - 1)
        + [blocks(parts)]
        + sems(parts),
    )
    grads, grad_1 = results[:parts], results[parts]
    *forward_1, grad_1 = lax.optimization_barrier((*forward_1, grad_1))
    out_1 = (acts[reach].astype(F32) + band_sum(forward_1, [(1, 1)])).astype(BF16)

    results = stage(starts, acts, gains, inverse, grads, weights, False, True)
    backward_0, projection, saved = results[:parts], results[parts], results[parts + 1 :]
    (summed,) = linked(sum_kernel, 3, [projection], [column], stats(count - 1) + sems(count - 1))
    scaled = band_sum(backward_0, [(0, 0)]) * gain[0:1, :]
    normed = acts[reach].astype(F32) * inverse
    grad_0 = (grads[reach].astype(F32) + inverse * (scaled - normed * (summed / D))).astype(BF16)
    gate_grads, up_grads, down_grads = weight_grads(
        starts, acts, gains, inverse, grads, saved, weights
    )
    return (
        jnp.where(first, act_1, out_1)[None],
        jnp.where(first, grad_0, grad_1)[None],
        gate_grads,
        up_grads,
        down_grads,
    )


def solution(mesh):
    return jax.shard_map(
        shards,
        mesh=mesh,
        in_specs=(
            P(None, "tp"),
            P(None, "tp"),
            P(("sweep", "pp"), "tp"),
            P(("sweep", "pp"), "tp", None, None),
            P(("sweep", "pp"), "tp", None, None),
            P(("sweep", "pp"), "tp", None, None),
            P(("sweep", "pp"), "tp"),
            P("sweep"),
        ),
        out_specs=(
            P(("sweep", "pp"), None, "tp"),
            P(("sweep", "pp"), None, "tp"),
            P(("sweep", "pp"), "tp", None, None),
            P(("sweep", "pp"), "tp", None, None),
            P(("sweep", "pp"), "tp", None, None),
        ),
        check_vma=False,
    )
```

```python
import functools

import jax
import jax.numpy as jnp
from jax import lax
from jax.experimental import pallas as pl
from jax.experimental.pallas import tpu as pltpu
from jax.sharding import PartitionSpec as P

D = 8192
BLK = 256
T_MB = 128
KB = 8
BAND = 2048
EPSILON = 1e-05
VMEM_LIMIT = 56 * 1024 * 1024
F32 = jnp.float32
BF16 = jnp.bfloat16


def dot(a, b):
    return jnp.dot(a, b, preferred_element_type=F32)


def dot_t(a, b):
    return lax.dot_general(a, b, (((1,), (1,)), ((), ())), preferred_element_type=F32)


def band_of(starts_ref, h):
    return pl.ds(pl.multiple_of(starts_ref[h] * BLK, BLK), BAND)


def fill_normed(normed, act_parts, gain_parts, inverse):
    width = act_parts[0].shape[1]
    for i, (act, gain) in enumerate(zip(act_parts, gain_parts)):
        normed[:, i * width : (i + 1) * width] = (
            act[...].astype(F32) * inverse[...] * gain[0:1, :]
        ).astype(BF16)


def emit_parts(total, outs):
    width = outs[0].shape[1]
    for i, out in enumerate(outs):
        out[...] = total[:, i * width : (i + 1) * width].astype(out.dtype)


def stage_kernel(parts, with_forward, with_backward, with_save, starts_ref, *refs):
    refs = list(refs)

    def take(n):
        got = refs[:n]
        del refs[:n]
        return got

    act_parts = take(parts)
    gain_parts = take(parts)
    (inverse,) = take(1)
    grad_parts = take(parts) if with_backward else []
    gate_w, up_w, down_w = take(3)
    forward_outs = take(parts) if with_forward else []
    if with_backward:
        backward_outs = take(parts)
        (projection,) = take(1)
    if with_save:
        hidden_out, gate_out, up_out = take(3)
    (normed,) = take(1)
    if with_forward:
        (forward_total,) = take(1)
    if with_backward:
        grads, backward_total = take(2)

    h = pl.program_id(0)

    @pl.when(h == 0)
    def _():
        fill_normed(normed, act_parts, gain_parts, inverse)
        if with_forward:
            forward_total[...] = jnp.zeros_like(forward_total)
        if with_backward:
            width = grad_parts[0].shape[1]
            for i, grad in enumerate(grad_parts):
                grads[:, i * width : (i + 1) * width] = grad[...]
            backward_total[...] = jnp.zeros_like(backward_total)

    columns = band_of(starts_ref, h)
    band_vals = normed[:, columns]
    gate = dot(band_vals, gate_w[...])
    up = dot(band_vals, up_w[...])
    sig = jax.nn.sigmoid(gate)
    silu = gate * sig
    hidden = (silu * up).astype(BF16)
    if with_forward:
        forward_total[:, columns] += dot(hidden, down_w[...])
    if with_backward:
        grad_hidden = dot_t(grads[:, columns], down_w[...])
        grad_gate = (grad_hidden * up * sig * (1.0 + gate * (1.0 - sig))).astype(BF16)
        grad_up = (grad_hidden * silu).astype(BF16)
        backward_total[:, columns] += dot_t(grad_gate, gate_w[...]) + dot_t(grad_up, up_w[...])
    if with_save:
        hidden_out[...] = hidden
        gate_out[...] = grad_gate
        up_out[...] = grad_up

    @pl.when(h == pl.num_programs(0) - 1)
    def _():
        if with_forward:
            emit_parts(forward_total, forward_outs)
        if with_backward:
            emit_parts(backward_total, backward_outs)
            width = act_parts[0].shape[1]
            products = jnp.zeros((projection.shape[0], 1), F32)
            for i, (act, gain) in enumerate(zip(act_parts, gain_parts)):
                scaled = backward_total[:, i * width : (i + 1) * width] * gain[0:1, :]
                products += jnp.sum(
                    scaled * (act[...].astype(F32) * inverse[...]), axis=1, keepdims=True
                )
            projection[...] = products


MESH = pl.DeviceIdType.MESH


def to_row(column):
    return jnp.broadcast_to(column, (column.shape[0], 128)).T[0:8, :]


def to_column(row):
    return jnp.broadcast_to(row[0:1, :], (128, row.shape[1])).T[:, 0:1]


def place():
    return lax.axis_index("tp"), lax.axis_index("pp"), lax.axis_size("tp")


def shifted(position, by, count):
    return lax.rem(position + (by % count), count)


def greet(sections=2):
    position, section, count = place()
    barrier = pltpu.get_barrier_semaphore()
    for j in range(count):
        for other in range(sections):
            if j > 0 or other > 0:
                pl.semaphore_signal(
                    barrier,
                    inc=1,
                    device_id={
                        "tp": shifted(position, j, count),
                        "pp": lax.rem(section + other, 2),
                    },
                    device_id_type=MESH,
                )
    pl.semaphore_wait(barrier, sections * count - 1)


def copies_to(sources, slots, send, recv, strides, section):
    position, _, count = place()
    return [
        pltpu.make_async_remote_copy(
            src_ref=source,
            dst_ref=slots.at[i],
            send_sem=send.at[i],
            recv_sem=recv.at[i],
            device_id={"tp": shifted(position, by, count), "pp": section},
            device_id_type=MESH,
        )
        for i, (source, by) in enumerate(zip(sources, strides))
    ]


def start_all(copies):
    for copy in copies:
        copy.start()


def others(reach):
    return [s for s in range(-reach, reach + 1) if s != 0]


def first_kernel(reach, tokens, gain, *refs):
    parts = 2 * reach + 1
    outs, gain_outs, inverse = refs[:parts], refs[parts : 2 * parts], refs[2 * parts]
    slots, gain_slots, row, rows, s1, r1, s2, r2, s3, r3 = refs[2 * parts + 1 :]
    _, section, count = place()
    strides = [-s for s in others(reach)]
    greet(1)
    moved = copies_to([tokens] * len(strides), slots, s1, r1, strides, section)
    moved_gain = copies_to([gain] * len(strides), gain_slots, s2, r2, strides, section)
    moved_row = copies_to([row] * (count - 1), rows, s3, r3, list(range(1, count)), section)
    start_all(moved_gain)
    outs[reach][...] = tokens[...]
    gain_outs[reach][...] = gain[...]

    @pl.when(section == 0)
    def _():
        start_all(moved)
        act = tokens[...].astype(F32)
        row[...] = to_row(jnp.sum(act * act, axis=1, keepdims=True))
        start_all(moved_row)
        for copy in moved_row + moved:
            copy.wait()
        total = row[...]
        for j in range(count - 1):
            total += rows[j]
        inverse[...] = lax.rsqrt(to_column(total) / D + EPSILON)
        for i, s in enumerate(others(reach)):
            outs[reach + s][...] = slots[i]

    @pl.when(section != 0)
    def _():
        inverse[...] = jnp.zeros_like(inverse)
        for s in others(reach):
            outs[reach + s][...] = jnp.zeros_like(outs[reach + s])

    for copy in moved_gain:
        copy.wait()
    for i, s in enumerate(others(reach)):
        gain_outs[reach + s][...] = gain_slots[i]


def sum_kernel(projection, summed, row, rows, send, recv):
    _, section, count = place()
    greet(1)
    row[...] = to_row(projection[...])
    moved = copies_to([row] * (count - 1), rows, send, recv, list(range(1, count)), section)
    start_all(moved)
    for copy in moved:
        copy.wait()
    total = row[...]
    for j in range(count - 1):
        total += rows[j]
    summed[...] = to_column(total)


def act_kernel(reach, *refs):
    parts = 2 * reach + 1
    pieces, own, inverse_0 = refs[:parts], refs[parts : 2 * parts], refs[2 * parts]
    outs, act_1, inverse = refs[2 * parts + 1 : 3 * parts + 1], refs[3 * parts + 1], refs[3 * parts + 2]
    slots, act_slots, row, rows, s1, r1, s2, r2, s3, r3 = refs[3 * parts + 3 :]
    _, section, count = place()
    around = others(reach)
    greet()
    moved = copies_to([pieces[reach + s] for s in around], slots, s1, r1, around, section)
    back = [-s for s in range(-reach, reach + 1)]
    moved_act = copies_to([act_1] * parts, act_slots, s2, r2, back, 1)
    moved_row = copies_to([row] * count, rows, s3, r3, list(range(count)), 1)

    @pl.when(section == 0)
    def _():
        start_all(moved)
        for copy in moved:
            copy.wait()
        total = pieces[reach][...]
        for i in range(len(around)):
            total += slots[i].astype(F32)
        result = (own[reach][...].astype(F32) + total).astype(BF16)
        act_1[...] = result
        start_all(moved_act)
        wide = result.astype(F32)
        row[...] = to_row(jnp.sum(wide * wide, axis=1, keepdims=True))
        start_all(moved_row)
        inverse[...] = inverse_0[...]
        for i in range(parts):
            outs[i][...] = own[i][...]
        for copy in moved_act + moved_row:
            copy.wait_send()

    @pl.when(section != 0)
    def _():
        act_1[...] = jnp.zeros_like(act_1)
        for copy in moved_row + moved_act:
            copy.wait_recv()
        total = rows[0]
        for j in range(1, count):
            total += rows[j]
        inverse[...] = lax.rsqrt(to_column(total) / D + EPSILON)
        for i in range(parts):
            outs[i][...] = act_slots[i]


def grad_kernel(reach, source, hand_on, *refs):
    parts = 2 * reach + 1
    pieces, own = refs[:parts], refs[parts : 2 * parts]
    projection, act, gain, inverse = refs[2 * parts : 2 * parts + 4]
    refs = refs[2 * parts + 4 :]
    outs = ()
    if hand_on:
        outs, refs = refs[:parts], refs[parts:]
    grad, slots, row, rows, s1, r1, s3, r3 = refs[:8]
    _, section, count = place()
    around = others(reach)
    greet()
    moved = copies_to([pieces[reach + s] for s in around], slots, s1, r1, around, section)
    moved_row = copies_to([row] * (count - 1), rows, s3, r3, list(range(1, count)), section)
    if hand_on:
        grad_slots, s2, r2 = refs[8:]
        back = [-s for s in range(-reach, reach + 1)]
        moved_grad = copies_to([grad] * parts, grad_slots, s2, r2, back, 1 - source)

    @pl.when(section == source)
    def _():
        start_all(moved)
        row[...] = to_row(projection[...])
        start_all(moved_row)
        for copy in moved_row + moved:
            copy.wait()
        summed = row[...]
        for j in range(count - 1):
            summed += rows[j]
        total = pieces[reach][...]
        for i in range(len(around)):
            total += slots[i].astype(F32)
        scale = inverse[...]
        normed = act[...].astype(F32) * scale
        mean = to_column(summed) / D
        grad[...] = (
            own[reach][...].astype(F32) + scale * (total * gain[0:1, :] - normed * mean)
        ).astype(BF16)
        if hand_on:
            start_all(moved_grad)
            for i in range(parts):
                outs[i][...] = own[i][...]
            for copy in moved_grad:
                copy.wait_send()

    @pl.when(section != source)
    def _():
        grad[...] = jnp.zeros_like(grad)
        if hand_on:
            for copy in moved_grad:
                copy.wait_recv()
            for i in range(parts):
                outs[i][...] = grad_slots[i]


def sems(*counts):
    return [pltpu.SemaphoreType.DMA((n,)) for n in counts for _ in range(2)]


def linked(kernel, identity, ins, shapes, scratch):
    vmem = pl.BlockSpec(memory_space=pltpu.VMEM)
    return pl.pallas_call(
        kernel,
        out_shape=shapes,
        in_specs=[vmem] * len(ins),
        out_specs=[vmem] * len(shapes),
        scratch_shapes=scratch,
        compiler_params=pltpu.CompilerParams(
            collective_id=identity, has_side_effects=True, vmem_limit_bytes=VMEM_LIMIT
        ),
    )(*ins)


def whole_spec(array):
    return pl.BlockSpec(array.shape, lambda h, s: (0,) * array.ndim)


def weight_specs():
    return [
        pl.BlockSpec((None, None, BAND, BLK), lambda h, s: (0, h, 0, 0)),
        pl.BlockSpec((None, None, BAND, BLK), lambda h, s: (0, h, 0, 0)),
        pl.BlockSpec((None, None, BLK, BAND), lambda h, s: (0, h, 0, 0)),
    ]


def stage(starts, acts, gains, inverse, grads, weights, with_forward, with_save):
    parts = len(acts)
    reach = parts // 2
    rows, width = acts[0].shape
    hidden_blocks = starts.shape[0]
    with_backward = grads is not None
    ins = list(acts) + list(gains) + [inverse] + (list(grads) if with_backward else [])
    kinds = [F32 if i == reach else BF16 for i in range(parts)]
    shapes = []
    if with_forward:
        shapes += [jax.ShapeDtypeStruct((rows, width), kind) for kind in kinds]
    if with_backward:
        shapes += [jax.ShapeDtypeStruct((rows, width), kind) for kind in kinds]
        shapes += [jax.ShapeDtypeStruct((rows, 1), F32)]
    out_specs = [whole_spec(shape) for shape in shapes]
    if with_save:
        shapes += [jax.ShapeDtypeStruct((rows, hidden_blocks * BLK), BF16)] * 3
        out_specs += [pl.BlockSpec((rows, BLK), lambda h, s: (0, h))] * 3
    scratch = [pltpu.VMEM((rows, parts * width), BF16)]
    if with_forward:
        scratch += [pltpu.VMEM((rows, parts * width), F32)]
    if with_backward:
        scratch += [pltpu.VMEM((rows, parts * width), BF16), pltpu.VMEM((rows, parts * width), F32)]
    products = 2 + (1 if with_forward else 0) + (3 if with_backward else 0)
    return pl.pallas_call(
        functools.partial(stage_kernel, parts, with_forward, with_backward, with_save),
        out_shape=shapes,
        grid_spec=pltpu.PrefetchScalarGridSpec(
            num_scalar_prefetch=1,
            grid=(hidden_blocks,),
            in_specs=[whole_spec(array) for array in ins] + weight_specs(),
            out_specs=out_specs,
            scratch_shapes=scratch,
        ),
        compiler_params=pltpu.CompilerParams(vmem_limit_bytes=VMEM_LIMIT),
        cost_estimate=pl.CostEstimate(
            flops=products * 2 * rows * BAND * BLK * hidden_blocks,
            bytes_accessed=6 * BAND * BLK * hidden_blocks,
            transcendentals=0,
        ),
    )(starts, *ins, *weights)


def weight_kernel(parts, starts_ref, *refs):
    act_parts = refs[:parts]
    gain_parts = refs[parts : 2 * parts]
    inverse = refs[2 * parts]
    grad_parts = refs[2 * parts + 1 : 3 * parts + 1]
    hidden, grad_gate, grad_up = refs[3 * parts + 1 : 3 * parts + 4]
    gate_out, up_out, down_out, normed_t, grads = refs[3 * parts + 4 :]
    h = pl.program_id(0)

    @pl.when(h == 0)
    def _():
        width = act_parts[0].shape[1]
        for i, (act, gain, grad) in enumerate(zip(act_parts, gain_parts, grad_parts)):
            grads[:, i * width : (i + 1) * width] = grad[...]
            normed = (act[...].astype(F32) * inverse[...] * gain[0:1, :]).astype(BF16)
            normed_t[i * width : (i + 1) * width, :] = normed.T

    columns = band_of(starts_ref, h)
    band_t = normed_t[columns, :]
    gate_out[...] = dot(band_t, grad_gate[...]).astype(BF16)
    up_out[...] = dot(band_t, grad_up[...]).astype(BF16)
    down_out[...] = dot(hidden[...].T, grads[:, columns]).astype(BF16)


def weight_grads(starts, acts, gains, inverse, grads, saved, weights):
    parts = len(acts)
    rows, width = acts[0].shape
    hidden_blocks = starts.shape[0]
    ins = list(acts) + list(gains) + [inverse] + list(grads)
    return pl.pallas_call(
        functools.partial(weight_kernel, parts),
        out_shape=[jax.ShapeDtypeStruct(w.shape, BF16) for w in weights],
        grid_spec=pltpu.PrefetchScalarGridSpec(
            num_scalar_prefetch=1,
            grid=(hidden_blocks,),
            in_specs=[whole_spec(array) for array in ins]
            + [pl.BlockSpec((rows, BLK), lambda h, s: (0, h))] * 3,
            out_specs=weight_specs(),
            scratch_shapes=[
                pltpu.VMEM((parts * width, rows), BF16),
                pltpu.VMEM((rows, parts * width), BF16),
            ],
        ),
        compiler_params=pltpu.CompilerParams(vmem_limit_bytes=VMEM_LIMIT),
        cost_estimate=pl.CostEstimate(
            flops=6 * rows * BAND * BLK * hidden_blocks,
            bytes_accessed=6 * BAND * BLK * hidden_blocks,
            transcendentals=0,
        ),
    )(starts, *ins, *saved)


def shards(tokens, cotangent, norm_gain, gate_band, up_band, down_band, offsets, counts):
    width = tokens.shape[1]
    blocks_dev = width // BLK
    reach = (KB // 2 - 1 + blocks_dev) // blocks_dev
    section = lax.axis_index("pp")
    position = lax.axis_index("tp")
    count = lax.axis_size("tp")
    sections = lax.axis_size("pp")
    first = section == 0
    starts = jnp.mod(offsets[0] - (position - reach) * blocks_dev, D // BLK)
    weights = (gate_band, up_band, down_band)
    strides = [s for s in range(-reach, reach + 1)]

    def move(value, by, pairs):
        perm = [
            (i * sections + source, (i + by) % count * sections + target)
            for source, target in pairs
            for i in range(count)
        ]
        return lax.ppermute(value, ("tp", "pp"), perm)

    def band_sum(pieces, pairs):
        total = pieces[reach]
        for i, s in enumerate(strides):
            if s != 0:
                total = total + move(pieces[i], s, pairs).astype(F32)
        return total

    row_ids = jnp.arange(tokens.shape[0], dtype=jnp.int32)
    valid = row_ids % T_MB < jnp.repeat(counts, T_MB, total_repeat_length=tokens.shape[0])
    cot = jnp.where(valid[:, None], cotangent, jnp.zeros((), BF16))

    rows = tokens.shape[0]
    parts = len(strides)
    near = parts - 1
    block = jax.ShapeDtypeStruct((rows, width), BF16)
    column = jax.ShapeDtypeStruct((rows, 1), F32)
    gain = jnp.broadcast_to(norm_gain.astype(F32), (8, width))
    gain_shape = jax.ShapeDtypeStruct(gain.shape, F32)

    def blocks(n):
        return pltpu.VMEM((n, rows, width), BF16)

    def stats(n):
        return [pltpu.VMEM((8, rows), F32), pltpu.VMEM((n, 8, rows), F32)]

    results = linked(
        functools.partial(first_kernel, reach),
        0,
        [tokens, gain],
        [block] * parts + [gain_shape] * parts + [column],
        [blocks(near), pltpu.VMEM((near, 8, width), F32)]
        + stats(count - 1)
        + sems(near, near, count - 1),
    )
    acts_0, gains, inverse_0 = results[:parts], results[parts : 2 * parts], results[-1]
    late_cot, inverse_0 = lax.optimization_barrier((cot, inverse_0))
    own = [cot if s == 0 else move(late_cot, -s, [(1, 1)]) for s in strides]

    pieces = stage(starts, acts_0, gains, inverse_0, None, weights, True, False)
    results = linked(
        functools.partial(act_kernel, reach),
        1,
        [*pieces, *acts_0, inverse_0],
        [block] * parts + [block, column],
        [blocks(near), blocks(parts)] + stats(count) + sems(near, parts, count),
    )
    acts, act_1, inverse = results[:parts], results[parts], results[parts + 1]

    results = stage(starts, acts, gains, inverse, own, weights, True, False)
    forward_1, backward_1, projection = results[:parts], results[parts : 2 * parts], results[-1]
    results = linked(
        functools.partial(grad_kernel, reach, 1, True),
        2,
        [*backward_1, *own, projection, acts[reach], gain, inverse],
        [block] * parts + [block],
        [blocks(near)]
        + stats(count - 1)
        + sems(near, count - 1)
        + [blocks(parts)]
        + sems(parts),
    )
    grads, grad_1 = results[:parts], results[parts]
    *forward_1, grad_1 = lax.optimization_barrier((*forward_1, grad_1))
    out_1 = (acts[reach].astype(F32) + band_sum(forward_1, [(1, 1)])).astype(BF16)

    results = stage(starts, acts, gains, inverse, grads, weights, False, True)
    backward_0, projection, saved = results[:parts], results[parts], results[parts + 1 :]
    gate_grads, up_grads, down_grads = weight_grads(
        starts, acts, gains, inverse, grads, saved, weights
    )
    projection, gate_grads = lax.optimization_barrier((projection, gate_grads))
    (summed,) = linked(sum_kernel, 3, [projection], [column], stats(count - 1) + sems(count - 1))
    scaled = band_sum(backward_0, [(0, 0)]) * gain[0:1, :]
    normed = acts[reach].astype(F32) * inverse
    grad_0 = (grads[reach].astype(F32) + inverse * (scaled - normed * (summed / D))).astype(BF16)
    return (
        jnp.where(first, act_1, out_1)[None],
        jnp.where(first, grad_0, grad_1)[None],
        gate_grads,
        up_grads,
        down_grads,
    )


def solution(mesh):
    return jax.shard_map(
        shards,
        mesh=mesh,
        in_specs=(
            P(None, "tp"),
            P(None, "tp"),
            P(("sweep", "pp"), "tp"),
            P(("sweep", "pp"), "tp", None, None),
            P(("sweep", "pp"), "tp", None, None),
            P(("sweep", "pp"), "tp", None, None),
            P(("sweep", "pp"), "tp"),
            P("sweep"),
        ),
        out_specs=(
            P(("sweep", "pp"), None, "tp"),
            P(("sweep", "pp"), None, "tp"),
            P(("sweep", "pp"), "tp", None, None),
            P(("sweep", "pp"), "tp", None, None),
            P(("sweep", "pp"), "tp", None, None),
        ),
        check_vma=False,
    )
```
